32 devices in a mesh: orb: 8 (over z, x), comp: 4 (over y, core).
Axes of the slice: x: 2, y: 2, z: 4, core: 2. Of those that a mesh axis runs over, the one named last changes fastest.
Arguments:
- psi: bfloat16 [512, 4, 64, 128], P('orb', None, 'comp'), may hold values from -16 to 16
- region_start: int32 [512], replicated, may hold values from 0 to 31
- region_len: int32 [512], replicated, may hold values from 16 to 32
- fine_mask: int32 [64, 8], P('comp'), may hold values 0 or 1
- occupation: int32 [512], replicated, may hold values from 0 to 2
- kinetic_taps: bfloat16 [29, 4, 4], replicated, may hold values from -0.5 to 0.5
- magic_taps: bfloat16 [16, 4], replicated, may hold values from -0.75 to 0.75
- external: float32 [64, 128], P('comp'), may hold values from -12 to 12
Outputs:
- density: float32 [64, 128], P('comp', 'orb')
- psi_next: bfloat16 [512, 4, 64, 128], P(None, None, 'comp', 'orb')
The draws below stay inside these ranges and needn't reach their ends.
Inputs may be any that keep to these rules, and one draw needn't show every extreme that they name: region_start + region_len <= 64.
All inputs are finite; a program needn't handle non-finite values. No bound on the sum of `fine_mask` on one device may be relied on, other than what follows from the above.
Results may differ from the reference program's by a relative error of at most 0.012.
Values may be sent and summed in bfloat16 or wider, within the bound.
No kernel may reach another device: no remote copies, remote signals or barrier semaphores. Data moves between devices by JAX's collectives and lax.ppermute only.
A program may use at most 128 MiB of HBM per device.

```python
import math
import jax
import jax.numpy as jnp
from jax import lax

CH = 4
TAPS = 29
MTAPS = 16
ZB = 16
ORB_DEV = 64
XD = 16
ZP = 16
NORB = 512
GX = 64
GZ = 128
NZB = 8
GRID = 8192
N_ORB = 8


def draw_psi(key, part):
    key_scale = jax.random.fold_in(key, 71)
    key_noise = jax.random.fold_in(key, 72)
    levels = jax.random.uniform(key_scale, (NORB, 1, GX // XD, 1, GZ // ZP, 1), jnp.float32) * math.log(16.0)
    amplitude = jnp.exp(levels)
    amplitude = amplitude / jnp.sqrt(jnp.mean(amplitude * amplitude, axis=(2, 4), keepdims=True))
    shape = (NORB, CH, GX // XD, XD, GZ // ZP, ZP)
    noise = jnp.clip(jax.random.normal(key_noise, shape, jnp.float32), -6.0, 6.0)
    values = (amplitude * noise).reshape(NORB, CH, GX, GZ)
    return values.astype(jnp.bfloat16)


def set_ends(array, rng, least, largest):
    dims = array.shape
    spot = [jax.random.randint(jax.random.fold_in(rng, axis), (), 0, dims[axis]) for axis in range(len(dims))]
    array = array.at[tuple(spot)].set(least)
    longest = dims.index(max(dims))
    spot[longest] = (spot[longest] + 1) % dims[longest]
    return array.at[tuple(spot)].set(largest)


def block_levels(key, shape, cuts, smallest, largest):
    def one(axis_at, blocks):
        heights = jax.random.uniform(jax.random.fold_in(jax.random.fold_in(key, 6), axis_at), (blocks,), jnp.float32, smallest / len(cuts), largest / len(cuts))
        return jnp.repeat(jnp.exp(heights), shape[axis_at] // blocks).reshape((-1,) + (1,) * (len(shape) - axis_at - 1))

    gain = one(*cuts[0])
    for cut in cuts[1:]:
        gain = gain * one(*cut)
    return gain


def centred(own_key, dims, deviation, most, cuts=(), kind=jnp.bfloat16):
    array = deviation * jax.random.normal(own_key, dims, jnp.float32)
    if cuts:
        array = array * block_levels(own_key, dims, cuts, -0.22, 0.18)
    return jnp.clip(array, -most, most).astype(kind)


def setup_inputs(seed: int = 0) -> dict:
    keys = jax.random.split(jax.random.key(seed), 9)
    psi = draw_psi(jax.random.fold_in(keys[8], 71), 0)
    region_start = set_ends(jax.random.randint(keys[1], (NORB,), 0, GX // 2), jax.random.fold_in(keys[1], 1), 0, (GX // 2) - 1).astype(jnp.int32)
    region_len = set_ends(jax.random.randint(keys[2], (NORB,), GX // 4, GX // 2 + 1), jax.random.fold_in(keys[2], 1), GX // 4, (GX // 2 + 1) - 1).astype(jnp.int32)
    fine_mask = set_ends((jax.random.randint(keys[3], (GX, NZB), 0, 2) < 1).astype(jnp.int32), jax.random.fold_in(keys[3], 1), 0, 1)
    occupation = set_ends(jax.random.randint(keys[4], (NORB,), 0, 3), jax.random.fold_in(keys[4], 1), 0, 2).astype(jnp.int32)
    kinetic_taps = centred(keys[5], (TAPS, CH, CH), (TAPS * CH) ** -0.5, 0.5)
    magic_taps = centred(keys[6], (MTAPS, CH), (MTAPS * CH) ** -0.5, 0.75)
    external = centred(keys[7], (GX, GZ), 2.0, 12.0, ((0, 4),), jnp.float32)
    return {"psi": psi, "region_start": region_start, "region_len": region_len, "fine_mask": fine_mask, "occupation": occupation, "kinetic_taps": kinetic_taps, "magic_taps": magic_taps, "external": external}


xc_factor = 0.98474502
step_length = 0.1
highest = lax.Precision.HIGHEST


def conv_planes(values, filter_taps):
    half = (filter_taps.shape[0] - 1) // 2
    padded = jnp.pad(values, ((0, 0), (0, 0), (half, half), (0, 0)))
    total = jnp.zeros(values.shape, jnp.float32)
    for position in range(filter_taps.shape[0]):
        total = total + jnp.einsum("ed,bdxz->bexz", filter_taps[position], padded[:, :, position:position + GX, :], precision=highest)
    return total


def conv_depth(values, filter_taps):
    half = (filter_taps.shape[0] - 1) // 2
    padded = jnp.pad(values, ((0, 0), (0, 0), (0, 0), (half, half)))
    total = jnp.zeros(values.shape, jnp.float32)
    for position in range(filter_taps.shape[0]):
        total = total + jnp.einsum("ed,bdxz->bexz", filter_taps[position], padded[:, :, :, position:position + GZ], precision=highest)
    return total


def magic_forward(values, magic):
    padded = jnp.pad(values, ((0, 0), (0, 0), (0, 0), (14, 14)))
    total = jnp.zeros((values.shape[0], GX, GZ), jnp.float32)
    for position in range(MTAPS):
        total = total + jnp.einsum("d,bdxz->bxz", magic[position], padded[:, :, :, position + 7:position + 7 + GZ], precision=highest)
    return total


def magic_adjoint(weighted, magic):
    padded = jnp.pad(weighted, ((0, 0), (0, 0), (14, 14)))
    total = jnp.zeros((weighted.shape[0], CH, GX, GZ), jnp.float32)
    for position in range(MTAPS):
        total = total + magic[position][None, :, None, None] * padded[:, None, :, 21 - position:21 - position + GZ]
    return total


def reference(psi, region_start, region_len, fine_mask, occupation, kinetic_taps, magic_taps, external):
    planes = jnp.arange(GX).astype(jnp.int32)
    inside = (planes[None, :] >= region_start[:, None]) & (planes[None, :] < (region_start + region_len)[:, None])
    fine_cells = jnp.repeat(fine_mask, ZB, axis=1)
    channel_on = (jnp.arange(CH)[:, None, None] == 0) | (fine_cells[None] > 0)
    kinetic_f = kinetic_taps.astype(jnp.float32)
    magic_f = magic_taps.astype(jnp.float32)
    blocks_psi = psi.reshape(N_ORB, ORB_DEV, CH, GX, GZ)
    blocks_in = inside.reshape(N_ORB, ORB_DEV, GX)

    def first(pair):
        block_psi, block_in = pair
        support = block_in[:, None, :, None] & channel_on[None]
        masked = jnp.where(support, block_psi, jnp.zeros((), block_psi.dtype))
        return masked, magic_forward(masked.astype(jnp.float32), magic_f)

    masked, grid_values = lax.map(first, (blocks_psi, blocks_in))
    occupied = occupation.astype(jnp.float32).reshape(N_ORB, ORB_DEV)
    density = jnp.sum(occupied[:, :, None, None] * grid_values * grid_values, axis=(0, 1))
    potential = external - xc_factor * jnp.cbrt(density)

    def second(triple):
        block_masked, block_values, block_in = triple
        support = block_in[:, None, :, None] & channel_on[None]
        weighted = (potential[None] * block_values).astype(jnp.bfloat16)
        weighted = lax.optimization_barrier(weighted)
        values = block_masked.astype(jnp.float32)
        total = conv_planes(values, kinetic_f) + conv_depth(values, kinetic_f)
        total = total + magic_adjoint(weighted.astype(jnp.float32), magic_f)
        return jnp.where(support, total, jnp.zeros((), jnp.float32)).astype(jnp.bfloat16)

    applied = lax.map(second, (masked, grid_values, blocks_in))
    masked_rows = masked.reshape(NORB, -1)
    applied_rows = applied.reshape(NORB, -1)
    intersection = jnp.dot(masked_rows, masked_rows.T, preferred_element_type=jnp.float32) / GRID
    lagrange = jnp.dot(applied_rows, masked_rows.T, preferred_element_type=jnp.float32) / GRID
    gradient = applied_rows.astype(jnp.float32) - jnp.dot(lagrange.astype(jnp.bfloat16), masked_rows, preferred_element_type=jnp.float32)
    trial = (masked_rows.astype(jnp.float32) - step_length * gradient).astype(jnp.bfloat16)
    trial = lax.optimization_barrier(trial)
    following = 1.5 * trial.astype(jnp.float32) - 0.5 * jnp.dot(intersection.astype(jnp.bfloat16), trial, preferred_element_type=jnp.float32)
    return density, following.astype(jnp.bfloat16).reshape(NORB, CH, GX, GZ)
```

```python
import functools

import jax
import jax.numpy as jnp
from jax import lax
from jax.experimental import pallas as pl
from jax.experimental.pallas import tpu as pltpu
from jax.sharding import PartitionSpec as P

ZB = 16
LANES = 128
CHUNK = 16

xc_factor = 0.98474502
step_length = 0.1
f32 = jnp.float32
bf16 = jnp.bfloat16
VMEM = pl.BlockSpec(memory_space=pltpu.VMEM)
SMEM = pl.BlockSpec(memory_space=pltpu.SMEM)


def params(mib=40):
    return pltpu.CompilerParams(vmem_limit_bytes=mib * 2**20)


def band(window, length, shift, sign, taps):
    count = taps.shape[0]
    offset = sign * (jnp.arange(window)[:, None] - jnp.arange(length)[None, :]) + shift
    onehot = (offset[:, :, None] == jnp.arange(count)[None, None, :]).astype(bf16)
    return onehot


def depth_matrix(taps, cells):
    onehot = band(cells, cells, 14, 1, taps)
    kernel = jnp.einsum("jit,ted->djei", onehot, taps, preferred_element_type=f32).astype(bf16)
    ch = taps.shape[1]
    return kernel.reshape(ch * cells, ch * cells)


def plane_matrix(taps, slab):
    ch = taps.shape[1]
    parts = []
    for block in (-1, 0, 1):
        onehot = band(slab, slab, 14 + block * slab, 1, taps)
        part = jnp.einsum("jit,ted->eidj", onehot, taps, preferred_element_type=f32).astype(bf16)
        parts.append(part.reshape(ch * slab, ch * slab))
    return jnp.concatenate(parts, axis=1)


def magic_matrix(magic, cells):
    onehot = band(cells, cells, 7, 1, magic)
    kernel = jnp.einsum("jit,td->dji", onehot, magic, preferred_element_type=f32).astype(bf16)
    return kernel.reshape(magic.shape[1] * cells, cells)


def adjoint_matrix(magic, cells):
    onehot = band(cells, cells, 7, -1, magic)
    kernel = jnp.einsum("jit,te->jei", onehot, magic, preferred_element_type=f32).astype(bf16)
    return kernel.reshape(cells, magic.shape[1] * cells)


def spread(scratch, row, value):
    slab = value.shape[0]
    for tile in range(value.shape[1] // LANES):
        scratch[tile, pl.ds(pl.multiple_of(row, slab), slab), :] = value[
            :, tile * LANES : (tile + 1) * LANES
        ]


def pack(scratch, out_ref, rows, piece):
    pieces, groups, orbs, _ = out_ref.shape
    blocks = LANES // piece
    lane = lax.broadcasted_iota(jnp.int32, (CHUNK, LANES), 1) // piece

    def group(g, carry):
        for tile in range(pieces // blocks):
            for start in range(0, orbs, CHUNK):
                held = [
                    scratch[tile, pl.ds(start * rows + g * blocks + c, CHUNK, stride=rows), :]
                    for c in range(blocks)
                ]
                bit = 1
                while bit < blocks:
                    low_lane = (lane & bit) == 0
                    for c in range(blocks):
                        if c & bit:
                            continue
                        low, high = held[c], held[c | bit]
                        held[c] = jnp.where(low_lane, low, pltpu.roll(high, bit * piece, 1))
                        held[c | bit] = jnp.where(
                            low_lane, pltpu.roll(low, LANES - bit * piece, 1), high
                        )
                    bit *= 2
                for c in range(blocks):
                    out_ref[tile * blocks + c, g, pl.ds(start, CHUNK), :] = held[c].astype(bf16)
        return carry

    lax.fori_loop(0, groups, group, 0)


def mask_body(piece, where_ref, start_ref, len_ref, psi_ref, fine_ref, masked_ref, out_ref, scratch):
    orbs, channels, slab, cells = psi_ref.shape
    rows = channels * slab
    first_orbital, first_plane = where_ref[0], where_ref[1]
    plane = first_plane + lax.broadcasted_iota(jnp.int32, (slab, cells), 0)
    fine = fine_ref[...] > 0

    def one(o, carry):
        s = start_ref[first_orbital + o]
        inside = (plane >= s) & (plane < s + len_ref[first_orbital + o])
        both = inside & fine
        for e in range(channels):
            keep = inside if e == 0 else both
            value = jnp.where(keep, psi_ref[o, e].astype(f32), 0.0)
            masked_ref[o, e] = value.astype(bf16)
            spread(scratch, o * rows + e * slab, value)
        return carry

    lax.fori_loop(0, orbs, one, 0, unroll=4)
    pack(scratch, out_ref, rows, piece)


def density_body(where_ref, occ_ref, masked_ref, magic_ref, values_ref, density_ref):
    orbs, channels, slab, cells = masked_ref.shape
    first_orbital = where_ref[0]

    def chunk(k, total):
        o = pl.multiple_of(k * CHUNK, CHUNK)
        lhs = jnp.concatenate(
            [
                masked_ref[pl.ds(o, CHUNK), d].reshape(CHUNK * slab, cells)
                for d in range(channels)
            ],
            axis=1,
        )
        result = jnp.dot(lhs, magic_ref[...], preferred_element_type=f32)
        values_ref[pl.ds(o, CHUNK)] = result.reshape(CHUNK, slab, cells)
        for i in range(CHUNK):
            part = result[i * slab : (i + 1) * slab]
            total = total + occ_ref[first_orbital + o + i].astype(f32) * part * part
        return total

    density_ref[...] = lax.fori_loop(0, orbs // CHUNK, chunk, jnp.zeros((slab, cells), f32))


def kinetic_body(
    where_ref, start_ref, len_ref, masked_ref, before_ref, after_ref, depth_ref, plane_ref, out_ref
):
    orbs, channels, slab, cells = masked_ref.shape
    rows = channels * slab

    def chunk(k, carry):
        o = pl.multiple_of(k * CHUNK, CHUNK)
        lhs = jnp.concatenate(
            [
                masked_ref[pl.ds(o, CHUNK), d].reshape(CHUNK * slab, cells)
                for d in range(channels)
            ],
            axis=1,
        )
        along_z = jnp.dot(lhs, depth_ref[...], preferred_element_type=f32)
        for i in range(0, CHUNK, 2):
            window = jnp.concatenate(
                [
                    jnp.concatenate(
                        [
                            ref[o + i + b].reshape(rows, cells)
                            for ref in (before_ref, masked_ref, after_ref)
                        ],
                        axis=0,
                    )
                    for b in range(2)
                ],
                axis=1,
            )
            along_x = jnp.dot(plane_ref[...], window, preferred_element_type=f32)
            for b in range(2):
                for e in range(channels):
                    out_ref[o + i + b, e] = (
                        along_x[e * slab : (e + 1) * slab, b * cells : (b + 1) * cells]
                        + along_z[
                            (i + b) * slab : (i + b + 1) * slab, e * cells : (e + 1) * cells
                        ]
                    )
        return carry

    lax.fori_loop(0, orbs // CHUNK, chunk, 0)


def applied_body(
    piece,
    where_ref,
    start_ref,
    len_ref,
    kinetic_ref,
    values_ref,
    potential_ref,
    fine_ref,
    adjoint_ref,
    out_ref,
    scratch,
):
    orbs, channels, slab, cells = kinetic_ref.shape
    rows = channels * slab
    first_orbital, first_plane = where_ref[0], where_ref[1]
    plane = first_plane + lax.broadcasted_iota(jnp.int32, (slab, cells), 0)
    fine = fine_ref[...] > 0
    potential = potential_ref[...]

    def chunk(k, carry):
        o = pl.multiple_of(k * CHUNK, CHUNK)
        weighted = (potential[None] * values_ref[pl.ds(o, CHUNK)]).astype(bf16)
        back = jnp.dot(
            weighted.reshape(CHUNK * slab, cells), adjoint_ref[...], preferred_element_type=f32
        )
        for i in range(CHUNK):
            s = start_ref[first_orbital + o + i]
            inside = (plane >= s) & (plane < s + len_ref[first_orbital + o + i])
            both = inside & fine
            for e in range(channels):
                keep = inside if e == 0 else both
                value = (
                    kinetic_ref[o + i, e]
                    + back[i * slab : (i + 1) * slab, e * cells : (e + 1) * cells]
                )
                spread(scratch, (o + i) * rows + e * slab, jnp.where(keep, value, 0.0))
        return carry

    lax.fori_loop(0, orbs // CHUNK, chunk, 0)
    pack(scratch, out_ref, rows, piece)


def unpack(got_ref, rows_ref):
    sources, groups, orbs, lanes = got_ref.shape
    for i in range(sources):
        for g in range(groups):
            rows_ref[pl.ds(i * orbs, orbs), pl.ds(g * lanes, lanes)] = got_ref[i, g]


def self_gram_body(got_ref, rows_ref, gram_ref):
    unpack(got_ref, rows_ref)
    gram_ref[...] = lax.dot_general(
        rows_ref[...], rows_ref[...], (((1,), (1,)), ((), ())), preferred_element_type=f32
    )


def cross_gram_body(got_ref, other_ref, rows_ref, gram_ref):
    unpack(got_ref, rows_ref)
    gram_ref[...] = lax.dot_general(
        rows_ref[...], other_ref[...], (((1,), (1,)), ((), ())), preferred_element_type=f32
    )


def update_body(masked_ref, applied_ref, lagrange_ref, inter_ref, out_ref):
    masked = masked_ref[...]
    gradient = applied_ref[...].astype(f32) - jnp.dot(
        lagrange_ref[...], masked, preferred_element_type=f32
    )
    trial = (masked.astype(f32) - step_length * gradient).astype(bf16)
    following = 1.5 * trial.astype(f32) - 0.5 * jnp.dot(
        inter_ref[...], trial, preferred_element_type=f32
    )
    out_ref[...] = following.T.astype(bf16)


def swap(value, axis, bit):
    count = lax.axis_size(axis)
    return lax.ppermute(value, axis, [(i, i ^ bit) for i in range(count)])


def bits_of(axis):
    bit, bits = 1, []
    while bit < lax.axis_size(axis):
        bits.append(bit)
        bit *= 2
    return bits


def half(value, upper):
    size = value.shape[0] // 2
    return lax.dynamic_slice_in_dim(value, upper * size, size, 0)


def sum_everywhere(part):
    steps = [("comp", b) for b in bits_of("comp")] + [("orb", b) for b in bits_of("orb")]
    halving = len(bits_of("comp")) + 1
    value = part
    taken = []
    for axis, bit in steps[:halving]:
        upper = (lax.axis_index(axis) // bit) % 2
        got = swap(half(value, 1 - upper).astype(bf16), axis, bit)
        value = half(value, upper) + got.astype(f32)
        taken.append((axis, bit, upper))
    for axis, bit in steps[halving:]:
        sent = value.astype(bf16)
        value = sent.astype(f32) + swap(sent, axis, bit).astype(f32)
    return value, taken


def give_everywhere(value, taken):
    for axis, bit, upper in reversed(taken):
        got = swap(value, axis, bit)
        value = jnp.where(
            upper == 0,
            jnp.concatenate([value, got], axis=0),
            jnp.concatenate([got, value], axis=0),
        )
    return value


def local(psi, region_start, region_len, fine_mask, occupation, kinetic_taps, magic_taps, external):
    orbs, channels, slab, cells = psi.shape
    orb_count = lax.axis_size("orb")
    comp_count = lax.axis_size("comp")
    orbitals = orbs * orb_count
    piece = cells // orb_count
    coefs = channels * slab * piece
    groups = coefs // LANES
    grid_cells = slab * comp_count * cells
    first_plane = lax.axis_index("comp") * slab
    first_cell = lax.axis_index("orb") * piece
    first_orbital = lax.axis_index("orb") * orbs
    where = jnp.stack([first_orbital, first_plane]).astype(jnp.int32)
    fine = jnp.repeat(fine_mask, ZB, axis=1)

    packed_shape = jax.ShapeDtypeStruct((orb_count, groups, orbs, LANES), bf16)
    scratch = pltpu.VMEM((cells // LANES, orbs * channels * slab, LANES), f32)
    masked, packed = pl.pallas_call(
        functools.partial(mask_body, piece),
        out_shape=(jax.ShapeDtypeStruct(psi.shape, bf16), packed_shape),
        in_specs=[SMEM, SMEM, SMEM, VMEM, VMEM],
        out_specs=(VMEM, VMEM),
        scratch_shapes=[scratch],
        compiler_params=params(),
        name="mask_pack",
    )(where, region_start, region_len, psi, fine)

    ends = comp_count - 1
    before = lax.ppermute(masked, "comp", [(i, i + 1) for i in range(ends)])
    after = lax.ppermute(masked, "comp", [(i + 1, i) for i in range(ends)])
    masked_got = lax.all_to_all(packed, "orb", split_axis=0, concat_axis=0, tiled=True)

    values, total = pl.pallas_call(
        density_body,
        out_shape=(
            jax.ShapeDtypeStruct((orbs, slab, cells), f32),
            jax.ShapeDtypeStruct((slab, cells), f32),
        ),
        in_specs=[SMEM, SMEM, VMEM, VMEM],
        out_specs=(VMEM, VMEM),
        compiler_params=params(),
        name="values_density",
    )(where, occupation, masked, magic_matrix(magic_taps, cells))
    for bit in bits_of("orb"):
        total = total + swap(total, "orb", bit)
    potential = external - xc_factor * jnp.cbrt(total)
    density = lax.dynamic_slice_in_dim(total, first_cell, piece, 1)

    kinetic = pl.pallas_call(
        kinetic_body,
        out_shape=jax.ShapeDtypeStruct(psi.shape, f32),
        in_specs=[SMEM, SMEM, SMEM, VMEM, VMEM, VMEM, VMEM, VMEM],
        out_specs=VMEM,
        compiler_params=params(),
        name="kinetic",
    )(
        where,
        region_start,
        region_len,
        masked,
        before,
        after,
        depth_matrix(kinetic_taps, cells),
        plane_matrix(kinetic_taps, slab),
    )

    packed_applied = pl.pallas_call(
        functools.partial(applied_body, piece),
        out_shape=packed_shape,
        in_specs=[SMEM, SMEM, SMEM, VMEM, VMEM, VMEM, VMEM, VMEM],
        out_specs=VMEM,
        scratch_shapes=[scratch],
        compiler_params=params(),
        name="applied_pack",
    )(
        where,
        region_start,
        region_len,
        kinetic,
        values,
        potential,
        fine,
        adjoint_matrix(magic_taps, cells),
    )
    applied_got = lax.all_to_all(packed_applied, "orb", split_axis=0, concat_axis=0, tiled=True)

    row_shape = jax.ShapeDtypeStruct((orbitals, coefs), bf16)
    gram_shape = jax.ShapeDtypeStruct((orbitals, orbitals), f32)
    masked_rows, inter_part = pl.pallas_call(
        self_gram_body,
        out_shape=(row_shape, gram_shape),
        in_specs=[VMEM],
        out_specs=(VMEM, VMEM),
        compiler_params=params(),
        name="intersection",
    )(masked_got)
    inter, taken = sum_everywhere(inter_part)
    inter_round = give_everywhere((inter / grid_cells).astype(bf16), taken)

    applied_rows, lagrange_part = pl.pallas_call(
        cross_gram_body,
        out_shape=(row_shape, gram_shape),
        in_specs=[VMEM, VMEM],
        out_specs=(VMEM, VMEM),
        compiler_params=params(),
        name="lagrange",
    )(applied_got, masked_rows)
    lagrange, taken = sum_everywhere(lagrange_part)
    lagrange_round = give_everywhere((lagrange / grid_cells).astype(bf16), taken)

    width = 256
    following = pl.pallas_call(
        update_body,
        grid=(coefs // width,),
        out_shape=jax.ShapeDtypeStruct((coefs, orbitals), bf16),
        in_specs=[
            pl.BlockSpec((orbitals, width), lambda k: (0, k)),
            pl.BlockSpec((orbitals, width), lambda k: (0, k)),
            pl.BlockSpec((orbitals, orbitals), lambda k: (0, 0)),
            pl.BlockSpec((orbitals, orbitals), lambda k: (0, 0)),
        ],
        out_specs=pl.BlockSpec((width, orbitals), lambda k: (k, 0)),
        compiler_params=params(),
        name="update",
    )(masked_rows, applied_rows, lagrange_round, inter_round)
    psi_next = following.reshape(channels, slab, piece, orbitals).transpose(3, 0, 1, 2)
    return (density, psi_next)


def solution(mesh):
    return jax.shard_map(
        local,
        mesh=mesh,
        in_specs=(
            P("orb", None, "comp", None),
            P(),
            P(),
            P("comp", None),
            P(),
            P(),
            P(),
            P("comp", None),
        ),
        out_specs=(P("comp", "orb"), P(None, None, "comp", "orb")),
        check_vma=False,
    )
```

```python
import functools

import jax
import jax.numpy as jnp
from jax import lax
from jax.experimental import pallas as pl
from jax.experimental.pallas import tpu as pltpu
from jax.sharding import PartitionSpec as P

ZB = 16
LANES = 128
CHUNK = 16
PAD = 8

xc_factor = 0.98474502
step_length = 0.1
f32 = jnp.float32
bf16 = jnp.bfloat16
VMEM = pl.BlockSpec(memory_space=pltpu.VMEM)
ANY = pl.BlockSpec(memory_space=pl.ANY)
SMEM = pl.BlockSpec(memory_space=pltpu.SMEM)


SMALL = pl.CostEstimate(flops=1024, bytes_accessed=1024, transcendentals=0)


def params(mib=20):
    return pltpu.CompilerParams(vmem_limit_bytes=mib * 2**20)


def band(window, length, shift, sign, taps):
    count = taps.shape[0]
    offset = sign * (jnp.arange(window)[:, None] - jnp.arange(length)[None, :]) + shift
    onehot = (offset[:, :, None] == jnp.arange(count)[None, None, :]).astype(bf16)
    return onehot


def depth_matrix(taps, cells):
    onehot = band(cells, cells, 14, 1, taps)
    kernel = jnp.einsum("jit,ted->djei", onehot, taps, preferred_element_type=f32).astype(bf16)
    ch = taps.shape[1]
    return kernel.reshape(ch * cells, ch * cells)


def plane_matrix(taps, slab):
    ch = taps.shape[1]
    parts = []
    for block in (-1, 0, 1):
        onehot = band(slab, slab, 14 + block * slab, 1, taps)
        part = jnp.einsum("jit,ted->eidj", onehot, taps, preferred_element_type=f32).astype(bf16)
        parts.append(part.reshape(ch * slab, ch * slab))
    return jnp.concatenate(parts, axis=1)


def magic_matrix(magic, cells):
    onehot = band(cells, cells, 7, 1, magic)
    kernel = jnp.einsum("jit,td->dji", onehot, magic, preferred_element_type=f32).astype(bf16)
    return kernel.reshape(magic.shape[1] * cells, cells)


def adjoint_matrix(magic, cells):
    onehot = band(cells, cells, 7, -1, magic)
    kernel = jnp.einsum("jit,te->jei", onehot, magic, preferred_element_type=f32).astype(bf16)
    return kernel.reshape(cells, magic.shape[1] * cells)


def spread(scratch, row, value):
    slab = value.shape[0]
    for tile in range(value.shape[1] // LANES):
        scratch[tile, pl.ds(pl.multiple_of(row, 8), slab), :] = value[
            :, tile * LANES : (tile + 1) * LANES
        ]


def pack(scratch, staged, out_ref, sems, orbs, rows, piece):
    pieces = staged.shape[0]
    blocks = LANES // piece
    pitch = scratch.shape[1] // orbs
    lane = lax.broadcasted_iota(jnp.int32, (CHUNK, LANES), 1) // piece

    def group(g, carry):
        for tile in range(pieces // blocks):
            for start in range(0, orbs, CHUNK):
                held = [
                    scratch[
                        tile, pl.ds(start * pitch + g * blocks + c, CHUNK, stride=pitch), :
                    ].astype(bf16)
                    for c in range(blocks)
                ]
                bit = 1
                while bit < blocks:
                    low_lane = (lane & bit) == 0
                    for c in range(blocks):
                        if c & bit:
                            continue
                        low, high = held[c], held[c | bit]
                        held[c] = jnp.where(low_lane, low, pltpu.roll(high, bit * piece, 1))
                        held[c | bit] = jnp.where(
                            low_lane, pltpu.roll(low, LANES - bit * piece, 1), high
                        )
                    bit *= 2
                for c in range(blocks):
                    row = pl.multiple_of(g * orbs + start, CHUNK)
                    staged[tile * blocks + c, pl.ds(row, CHUNK), :] = held[c]
        leave(g).start()
        return carry

    def leave(g):
        share = pl.ds(pl.multiple_of(g * orbs, CHUNK), orbs)
        return pltpu.make_async_copy(
            staged.at[:, share, :], out_ref.at[:, share, :], sems.at[g]
        )

    def finish(g, carry):
        leave(g).wait()
        return carry

    lax.fori_loop(0, rows // blocks, group, 0)
    lax.fori_loop(0, rows // blocks, finish, 0)


def fine_cells(fine_ref, cells):
    blocks = fine_ref.shape[0]
    spot = lax.broadcasted_iota(jnp.int32, (blocks, cells), 1) // ZB
    onehot = (spot == lax.broadcasted_iota(jnp.int32, (blocks, cells), 0)).astype(f32)
    wide = lax.dot_general(
        fine_ref[...].astype(f32), onehot, (((0,), (0,)), ((), ())), preferred_element_type=f32
    )
    return wide > 0.5


def region(table_ref, orbs, o):
    spot = lax.axis_index("orb") * orbs + o
    return table_ref[0, spot], table_ref[0, spot] + table_ref[1, spot]


def mask_body(
    piece,
    table_ref,
    psi_hbm,
    fine_hbm,
    magic_ref,
    masked_ref,
    out_ref,
    scratch,
    staged,
    psi_ref,
    fine_ref,
    sems,
    in_sems,
):
    orbs, channels, slab, cells = psi_ref.shape
    rows = channels * slab
    pitch = scratch.shape[1] // orbs

    def arrive(k):
        share = pl.ds(pl.multiple_of(k * CHUNK, CHUNK), CHUNK)
        return pltpu.make_async_copy(psi_hbm.at[share], psi_ref.at[share], in_sems.at[k])

    fine_copy = pltpu.make_async_copy(fine_hbm, fine_ref, in_sems.at[orbs // CHUNK])
    fine_copy.start()
    for k in range(orbs // CHUNK):
        arrive(k).start()
    first_orbital = lax.axis_index("orb") * orbs
    plane = lax.axis_index("comp") * slab + lax.broadcasted_iota(jnp.int32, (slab, cells), 0)
    fine_copy.wait()
    fine = fine_cells(fine_ref, cells)

    def chunk(k, total):
        o = pl.multiple_of(k * CHUNK, CHUNK)
        arrive(k).wait()
        for i in range(CHUNK):
            least, limit = region(table_ref, orbs, o + i)
            inside = (plane >= least) & (plane < limit)
            both = inside & fine
            for e in range(channels):
                keep = inside if e == 0 else both
                value = jnp.where(keep, psi_ref[o + i, e].astype(f32), 0.0)
                masked_ref[o + i, e] = value.astype(bf16)
                spread(scratch, (o + i) * pitch + e * slab, value)
        lhs = jnp.concatenate(
            [
                masked_ref[pl.ds(o, CHUNK), d].reshape(CHUNK * slab, cells)
                for d in range(channels)
            ],
            axis=1,
        )
        result = jnp.dot(lhs, magic_ref[...], preferred_element_type=f32)
        for i in range(CHUNK):
            part = result[i * slab : (i + 1) * slab]
            total = total + table_ref[2, first_orbital + o + i].astype(f32) * part * part
        return total

    density = lax.fori_loop(0, orbs // CHUNK, chunk, jnp.zeros((slab, cells), f32))
    coarse = density.astype(bf16)
    rest = (density - coarse.astype(f32)).astype(bf16)
    body = orbs * rows * piece // LANES
    for j in range(staged.shape[0]):
        row = body
        for part in (coarse, rest):
            for tile in range(cells // LANES):
                staged[j, row : row + slab, :] = part[:, tile * LANES : (tile + 1) * LANES]
                row += slab
    extra = pltpu.make_async_copy(
        staged.at[:, body:, :], out_ref.at[:, body:, :], sems.at[rows * piece // LANES]
    )
    extra.start()
    pack(scratch, staged, out_ref, sems, orbs, rows, piece)
    extra.wait()


def kinetic_body(
    masked_ref, before_ref, after_ref, depth_ref, plane_ref, magic_ref, out_ref, values_ref
):
    orbs, channels, slab, cells = masked_ref.shape
    rows = channels * slab

    def chunk(k, carry):
        o = pl.multiple_of(k * CHUNK, CHUNK)
        lhs = jnp.concatenate(
            [
                masked_ref[pl.ds(o, CHUNK), d].reshape(CHUNK * slab, cells)
                for d in range(channels)
            ],
            axis=1,
        )
        along_z = jnp.dot(lhs, depth_ref[...], preferred_element_type=f32)
        values_ref[pl.ds(o, CHUNK)] = jnp.dot(
            lhs, magic_ref[...], preferred_element_type=f32
        ).reshape(CHUNK, slab, cells)
        for i in range(0, CHUNK, 2):
            window = jnp.concatenate(
                [
                    jnp.concatenate(
                        [
                            ref[o + i + b].reshape(rows, cells)
                            for ref in (before_ref, masked_ref, after_ref)
                        ],
                        axis=0,
                    )
                    for b in range(2)
                ],
                axis=1,
            )
            along_x = jnp.dot(plane_ref[...], window, preferred_element_type=f32)
            for b in range(2):
                for e in range(channels):
                    out_ref[o + i + b, e] = (
                        along_x[e * slab : (e + 1) * slab, b * cells : (b + 1) * cells]
                        + along_z[
                            (i + b) * slab : (i + b + 1) * slab, e * cells : (e + 1) * cells
                        ]
                    )
        return carry

    lax.fori_loop(0, orbs // CHUNK, chunk, 0)


def applied_body(
    piece,
    table_ref,
    kinetic_ref,
    values_ref,
    potential_ref,
    fine_ref,
    adjoint_ref,
    out_ref,
    scratch,
    staged,
    sems,
):
    orbs, channels, slab, cells = kinetic_ref.shape
    rows = channels * slab
    pitch = scratch.shape[1] // orbs
    plane = lax.axis_index("comp") * slab + lax.broadcasted_iota(jnp.int32, (slab, cells), 0)
    fine = fine_cells(fine_ref, cells)
    potential = potential_ref[...]

    def chunk(k, carry):
        o = pl.multiple_of(k * CHUNK, CHUNK)
        weighted = (potential[None] * values_ref[pl.ds(o, CHUNK)]).astype(bf16)
        back = jnp.dot(
            weighted.reshape(CHUNK * slab, cells), adjoint_ref[...], preferred_element_type=f32
        )
        for i in range(CHUNK):
            least, limit = region(table_ref, orbs, o + i)
            inside = (plane >= least) & (plane < limit)
            both = inside & fine
            for e in range(channels):
                keep = inside if e == 0 else both
                value = (
                    kinetic_ref[o + i, e]
                    + back[i * slab : (i + 1) * slab, e * cells : (e + 1) * cells]
                )
                spread(scratch, (o + i) * pitch + e * slab, jnp.where(keep, value, 0.0))
        return carry

    lax.fori_loop(0, orbs // CHUNK, chunk, 0)
    pack(scratch, staged, out_ref, sems, orbs, rows, piece)


def unpack(got_ref, rows_ref):
    sources = got_ref.shape[0]
    orbs = rows_ref.shape[0] // sources
    for i in range(sources):
        for g in range(rows_ref.shape[1] // LANES):
            rows_ref[pl.ds(i * orbs, orbs), pl.ds(g * LANES, LANES)] = got_ref[
                i, g * orbs : (g + 1) * orbs, :
            ]


def gram_halves(left_ref, right_ref, kept_ref, sent_ref):
    half = kept_ref.shape[0]
    mine = lax.axis_index("comp") % 2
    for place, ref in ((mine, kept_ref), (1 - mine, sent_ref)):
        row = pl.multiple_of(place * half, half)
        ref[...] = lax.dot_general(
            left_ref[pl.ds(row, half), :],
            right_ref[...],
            (((1,), (1,)), ((), ())),
            preferred_element_type=f32,
        ).astype(ref.dtype)


def self_gram_body(got_ref, rows_ref, kept_ref, sent_ref):
    unpack(got_ref, rows_ref)
    gram_halves(rows_ref, rows_ref, kept_ref, sent_ref)


def cross_gram_body(got_ref, other_ref, rows_ref, kept_ref, sent_ref):
    unpack(got_ref, rows_ref)
    gram_halves(rows_ref, other_ref, kept_ref, sent_ref)


def update_body(masked_ref, applied_ref, lagrange_ref, inter_ref, out_ref):
    masked = masked_ref[...]
    gradient = applied_ref[...].astype(f32) - jnp.dot(
        lagrange_ref[...], masked, preferred_element_type=f32
    )
    trial = (masked.astype(f32) - step_length * gradient).astype(bf16)
    following = 1.5 * trial.astype(f32) - 0.5 * jnp.dot(
        inter_ref[...], trial, preferred_element_type=f32
    )
    out_ref[...] = following.astype(bf16).T


def swap(value, axis, bit):
    count = lax.axis_size(axis)
    return lax.ppermute(value, axis, [(i, i ^ bit) for i in range(count)])


def bits_of(axis):
    bit, bits = 1, []
    while bit < lax.axis_size(axis):
        bits.append(bit)
        bit *= 2
    return bits


def stages():
    comp, orb = bits_of("comp"), bits_of("orb")
    groups = [[("comp", comp[0])]]
    for index, bit in enumerate(comp[1:]):
        groups.append([("comp", bit), ("orb", orb[index])])
    return groups, [("orb", bit) for bit in orb[len(comp) - 1 :]]


def place(group):
    return sum(((lax.axis_index(a) // b) % 2) << k for k, (a, b) in enumerate(group))


def pass_on(value, group, distance):
    flips = {}
    for k, (axis, bit) in enumerate(group):
        if distance >> k & 1:
            flips[axis] = flips.get(axis, 0) ^ bit
    axes = tuple(a for a in ("orb", "comp") if a in flips)
    if len(axes) == 1:
        return swap(value, axes[0], flips[axes[0]])
    sizes = [lax.axis_size(a) for a in axes]
    pairs = []
    for i in range(sizes[0]):
        for j in range(sizes[1]):
            to = (i ^ flips[axes[0]], j ^ flips[axes[1]])
            pairs.append((i * sizes[1] + j, to[0] * sizes[1] + to[1]))
    return lax.ppermute(value, axes, pairs)


def add_partner(kept, sent):
    return kept + pass_on(sent, stages()[0][0], 1).astype(f32)


def share_out(value):
    for group in stages()[0][1:]:
        members = 1 << len(group)
        size = value.shape[0] // members
        me = place(group)
        sent = value.astype(bf16)
        total = lax.dynamic_slice_in_dim(value, me * size, size, 0)
        for distance in range(1, members):
            share = lax.dynamic_slice_in_dim(sent, (me ^ distance) * size, size, 0)
            total = total + pass_on(share, group, distance).astype(f32)
        value = total
    return value


def exchange(value, step):
    axis, bit = step
    sent = value.astype(bf16)
    return sent.astype(f32) + swap(sent, axis, bit).astype(f32)


def give_everywhere(value):
    for group in reversed(stages()[0]):
        members = 1 << len(group)
        size = value.shape[0]
        me = place(group)
        got = [value] + [pass_on(value, group, d) for d in range(1, members)]
        whole = jnp.zeros((members * size,) + value.shape[1:], value.dtype)
        for distance, block in enumerate(got):
            whole = lax.dynamic_update_slice_in_dim(whole, block, (me ^ distance) * size, 0)
        value = whole
    return value


def local(psi, region_start, region_len, fine_mask, occupation, kinetic_taps, magic_taps, external):
    orbs, channels, slab, cells = psi.shape
    orb_count = lax.axis_size("orb")
    comp_count = lax.axis_size("comp")
    orbitals = orbs * orb_count
    piece = cells // orb_count
    coefs = channels * slab * piece
    groups = coefs // LANES
    grid_cells = slab * comp_count * cells
    first_cell = lax.axis_index("orb") * piece
    table = jnp.stack([region_start, region_len, occupation])
    fine = fine_mask.T

    scratch = pltpu.VMEM((cells // LANES, orbs * (channels * slab + PAD), LANES), f32)
    body_rows = orbs * coefs // LANES
    extra = slab * (cells // LANES)
    magic_forward = magic_matrix(magic_taps, cells)
    packed_shape = (orb_count, body_rows + 2 * extra, LANES)
    masked, packed = pl.pallas_call(
        functools.partial(mask_body, piece),
        out_shape=(
            jax.ShapeDtypeStruct(psi.shape, bf16),
            jax.ShapeDtypeStruct(packed_shape, bf16),
        ),
        in_specs=[SMEM, ANY, ANY, VMEM],
        out_specs=(VMEM, ANY),
        scratch_shapes=[
            scratch,
            pltpu.VMEM(packed_shape, bf16),
            pltpu.VMEM(psi.shape, bf16),
            pltpu.VMEM(fine.shape, fine.dtype),
            pltpu.SemaphoreType.DMA((groups + 1,)),
            pltpu.SemaphoreType.DMA((orbs // CHUNK + 1,)),
        ],
        compiler_params=params(),
        name="mask_values_pack",
        cost_estimate=SMALL,
    )(table, psi, fine, magic_forward)

    ends = comp_count - 1
    before = lax.ppermute(masked, "comp", [(i, i + 1) for i in range(ends)])
    after = lax.ppermute(masked, "comp", [(i + 1, i) for i in range(ends)])
    masked_got = lax.all_to_all(packed, "orb", split_axis=0, concat_axis=0, tiled=True)
    parts = masked_got[:, body_rows:].reshape(orb_count * 2, cells // LANES, slab, LANES)
    total = jnp.sum(parts.astype(f32), axis=0).transpose(1, 0, 2).reshape(slab, cells)
    potential = external - xc_factor * jnp.cbrt(total)
    density = lax.dynamic_slice_in_dim(total, first_cell, piece, 1)

    kinetic, values = pl.pallas_call(
        kinetic_body,
        out_shape=(
            jax.ShapeDtypeStruct(psi.shape, f32),
            jax.ShapeDtypeStruct((orbs, slab, cells), f32),
        ),
        in_specs=[VMEM] * 6,
        out_specs=(VMEM, VMEM),
        compiler_params=params(),
        name="kinetic",
        cost_estimate=SMALL,
    )(
        masked,
        before,
        after,
        depth_matrix(kinetic_taps, cells),
        plane_matrix(kinetic_taps, slab),
        magic_forward,
    )

    packed_applied = pl.pallas_call(
        functools.partial(applied_body, piece),
        out_shape=jax.ShapeDtypeStruct((orb_count, body_rows, LANES), bf16),
        in_specs=[SMEM] + [VMEM] * 5,
        out_specs=ANY,
        scratch_shapes=[
            scratch,
            pltpu.VMEM((orb_count, body_rows, LANES), bf16),
            pltpu.SemaphoreType.DMA((groups,)),
        ],
        compiler_params=params(),
        name="applied_pack",
        cost_estimate=SMALL,
    )(
        table,
        kinetic,
        values,
        potential,
        fine,
        adjoint_matrix(magic_taps, cells),
    )
    applied_got = lax.all_to_all(packed_applied, "orb", split_axis=0, concat_axis=0, tiled=True)

    row_shape = jax.ShapeDtypeStruct((orbitals, coefs), bf16)
    kept_shape = jax.ShapeDtypeStruct((orbitals // 2, orbitals), f32)
    sent_shape = jax.ShapeDtypeStruct((orbitals // 2, orbitals), bf16)
    masked_rows, *inter_part = pl.pallas_call(
        self_gram_body,
        out_shape=(row_shape, kept_shape, sent_shape),
        in_specs=[VMEM],
        out_specs=(VMEM, VMEM, VMEM),
        compiler_params=params(),
        name="intersection",
        cost_estimate=SMALL,
    )(masked_got)
    inter = share_out(add_partner(*inter_part))

    applied_got, inter = lax.optimization_barrier((applied_got, inter))
    applied_rows, *lagrange_part = pl.pallas_call(
        cross_gram_body,
        out_shape=(row_shape, kept_shape, sent_shape),
        in_specs=[VMEM, VMEM],
        out_specs=(VMEM, VMEM, VMEM),
        compiler_params=params(),
        name="lagrange",
        cost_estimate=SMALL,
    )(applied_got, masked_rows)
    lagrange = share_out(add_partner(*lagrange_part))
    both = jnp.concatenate([lagrange, inter], axis=1)
    for step in stages()[1]:
        both = exchange(both, step)
    both = give_everywhere((both / grid_cells).astype(bf16))

    width = 512
    following = pl.pallas_call(
        update_body,
        grid=(coefs // width,),
        out_shape=jax.ShapeDtypeStruct((coefs, orbitals), bf16),
        in_specs=[
            pl.BlockSpec((orbitals, width), lambda k: (0, k)),
            pl.BlockSpec((orbitals, width), lambda k: (0, k)),
            pl.BlockSpec((orbitals, orbitals), lambda k: (0, 0)),
            pl.BlockSpec((orbitals, orbitals), lambda k: (0, 1)),
        ],
        out_specs=pl.BlockSpec((width, orbitals), lambda k: (k, 0)),
        compiler_params=params(),
        name="update",
        cost_estimate=SMALL,
    )(masked_rows, applied_rows, both, both)
    psi_next = following.reshape(channels, slab, piece, orbitals).transpose(3, 0, 1, 2)
    return (density, psi_next)


def solution(mesh):
    return jax.shard_map(
        local,
        mesh=mesh,
        in_specs=(
            P("orb", None, "comp", None),
            P(),
            P(),
            P("comp", None),
            P(),
            P(),
            P(),
            P("comp", None),
        ),
        out_specs=(P("comp", "orb"), P(None, None, "comp", "orb")),
        check_vma=False,
    )
```

```python
import functools

import jax
import jax.numpy as jnp
from jax import lax
from jax.experimental import pallas as pl
from jax.experimental.pallas import tpu as pltpu
from jax.sharding import PartitionSpec as P

ZB = 16
LANES = 128
CHUNK = 16
PAD = 8

xc_factor = 0.98474502
step_length = 0.1
f32 = jnp.float32
bf16 = jnp.bfloat16
VMEM = pl.BlockSpec(memory_space=pltpu.VMEM)
ANY = pl.BlockSpec(memory_space=pl.ANY)
SMEM = pl.BlockSpec(memory_space=pltpu.SMEM)


SMALL = pl.CostEstimate(flops=1024, bytes_accessed=1024, transcendentals=0)


def params(mib=20):
    return pltpu.CompilerParams(vmem_limit_bytes=mib * 2**20)


def band(window, length, shift, sign, taps):
    count = taps.shape[0]
    offset = sign * (jnp.arange(window)[:, None] - jnp.arange(length)[None, :]) + shift
    onehot = (offset[:, :, None] == jnp.arange(count)[None, None, :]).astype(bf16)
    return onehot


def depth_matrix(taps, cells):
    onehot = band(cells, cells, 14, 1, taps)
    kernel = jnp.einsum("jit,ted->djei", onehot, taps, preferred_element_type=f32).astype(bf16)
    ch = taps.shape[1]
    return kernel.reshape(ch * cells, ch * cells)


def plane_matrix(taps, slab):
    ch = taps.shape[1]
    parts = []
    for block in (-1, 0, 1):
        onehot = band(slab, slab, 14 + block * slab, 1, taps)
        part = jnp.einsum("jit,ted->eidj", onehot, taps, preferred_element_type=f32).astype(bf16)
        parts.append(part.reshape(ch * slab, ch * slab))
    return jnp.concatenate(parts, axis=1)


def magic_matrix(magic, cells):
    onehot = band(cells, cells, 7, 1, magic)
    kernel = jnp.einsum("jit,td->dji", onehot, magic, preferred_element_type=f32).astype(bf16)
    return kernel.reshape(magic.shape[1] * cells, cells)


def adjoint_matrix(magic, cells):
    onehot = band(cells, cells, 7, -1, magic)
    kernel = jnp.einsum("jit,te->jei", onehot, magic, preferred_element_type=f32).astype(bf16)
    return kernel.reshape(cells, magic.shape[1] * cells)


def spread(scratch, row, value):
    slab = value.shape[0]
    for tile in range(value.shape[1] // LANES):
        scratch[tile, pl.ds(pl.multiple_of(row, 8), slab), :] = value[
            :, tile * LANES : (tile + 1) * LANES
        ]


def pack(scratch, staged, orbs, rows, piece, copies=None):
    pieces = staged.shape[0]
    blocks = LANES // piece
    pitch = scratch.shape[1] // orbs
    lane = lax.broadcasted_iota(jnp.int32, (CHUNK, LANES), 1) // piece

    def group(g, carry):
        for tile in range(pieces // blocks):
            for start in range(0, orbs, CHUNK):
                held = [
                    scratch[
                        tile, pl.ds(start * pitch + g * blocks + c, CHUNK, stride=pitch), :
                    ].astype(bf16)
                    for c in range(blocks)
                ]
                bit = 1
                while bit < blocks:
                    low_lane = (lane & bit) == 0
                    for c in range(blocks):
                        if c & bit:
                            continue
                        low, high = held[c], held[c | bit]
                        held[c] = jnp.where(low_lane, low, pltpu.roll(high, bit * piece, 1))
                        held[c | bit] = jnp.where(
                            low_lane, pltpu.roll(low, LANES - bit * piece, 1), high
                        )
                    bit *= 2
                for c in range(blocks):
                    row = pl.multiple_of(g * orbs + start, CHUNK)
                    staged[tile * blocks + c, pl.ds(row, CHUNK), :] = held[c]
        if copies:
            leave(g).start()
        return carry

    def leave(g):
        out_ref, sems = copies
        share = pl.ds(pl.multiple_of(g * orbs, CHUNK), orbs)
        return pltpu.make_async_copy(
            staged.at[:, share, :], out_ref.at[:, share, :], sems.at[g]
        )

    def finish(g, carry):
        leave(g).wait()
        return carry

    lax.fori_loop(0, rows // blocks, group, 0)
    if copies:
        lax.fori_loop(0, rows // blocks, finish, 0)


def fine_cells(table_ref, slab, cells):
    x = lax.broadcasted_iota(jnp.int32, (slab, LANES), 0)
    block = lax.broadcasted_iota(jnp.int32, (slab, LANES), 1) // ZB
    tiles = []
    for tile in range(cells // LANES):
        held = jnp.zeros((slab, LANES), jnp.int32)
        for b in range(LANES // ZB):
            for p in range(slab):
                bit = table_ref[3 + tile * (LANES // ZB) + b, p]
                held = jnp.where((x == p) & (block == b), bit, held)
        tiles.append(held)
    return jnp.concatenate(tiles, axis=1) > 0


def region(table_ref, orbs, o):
    spot = lax.axis_index("orb") * orbs + o
    return table_ref[0, spot], table_ref[0, spot] + table_ref[1, spot]


def mask_body(
    piece,
    table_ref,
    psi_ref,
    magic_ref,
    masked_ref,
    out_ref,
    scratch,
    staged,
    sems,
):
    orbs, channels, slab, cells = psi_ref.shape
    rows = channels * slab
    pitch = scratch.shape[1] // orbs

    first_orbital = lax.axis_index("orb") * orbs
    plane = lax.axis_index("comp") * slab + lax.broadcasted_iota(jnp.int32, (slab, cells), 0)
    fine = fine_cells(table_ref, slab, cells)

    def chunk(k, total):
        o = pl.multiple_of(k * CHUNK, CHUNK)
        for i in range(CHUNK):
            least, limit = region(table_ref, orbs, o + i)
            inside = (plane >= least) & (plane < limit)
            both = inside & fine
            for e in range(channels):
                keep = inside if e == 0 else both
                value = jnp.where(keep, psi_ref[o + i, e].astype(f32), 0.0)
                masked_ref[o + i, e] = value.astype(bf16)
                spread(scratch, (o + i) * pitch + e * slab, value)
        lhs = jnp.concatenate(
            [
                masked_ref[pl.ds(o, CHUNK), d].reshape(CHUNK * slab, cells)
                for d in range(channels)
            ],
            axis=1,
        )
        result = jnp.dot(lhs, magic_ref[...], preferred_element_type=f32)
        for i in range(CHUNK):
            part = result[i * slab : (i + 1) * slab]
            total = total + table_ref[2, first_orbital + o + i].astype(f32) * part * part
        return total

    density = lax.fori_loop(0, orbs // CHUNK, chunk, jnp.zeros((slab, cells), f32))
    coarse = density.astype(bf16)
    rest = (density - coarse.astype(f32)).astype(bf16)
    body = orbs * rows * piece // LANES
    for j in range(staged.shape[0]):
        row = body
        for part in (coarse, rest):
            for tile in range(cells // LANES):
                staged[j, row : row + slab, :] = part[:, tile * LANES : (tile + 1) * LANES]
                row += slab
    extra = pltpu.make_async_copy(
        staged.at[:, body:, :], out_ref.at[:, body:, :], sems.at[rows * piece // LANES]
    )
    extra.start()
    pack(scratch, staged, orbs, rows, piece, (out_ref, sems))
    extra.wait()


def kinetic_body(
    masked_ref, before_ref, after_ref, depth_ref, plane_ref, magic_ref, out_ref
):
    orbs, channels, slab, cells = masked_ref.shape
    rows = channels * slab

    def chunk(k, carry):
        o = pl.multiple_of(k * CHUNK, CHUNK)
        lhs = jnp.concatenate(
            [
                masked_ref[pl.ds(o, CHUNK), d].reshape(CHUNK * slab, cells)
                for d in range(channels)
            ],
            axis=1,
        )
        along_z = jnp.dot(lhs, depth_ref[...], preferred_element_type=f32)
        out_ref[pl.ds(o, CHUNK), channels] = jnp.dot(
            lhs, magic_ref[...], preferred_element_type=f32
        ).reshape(CHUNK, slab, cells)
        for i in range(0, CHUNK, 2):
            window = jnp.concatenate(
                [
                    jnp.concatenate(
                        [
                            ref[o + i + b].reshape(rows, cells)
                            for ref in (before_ref, masked_ref, after_ref)
                        ],
                        axis=0,
                    )
                    for b in range(2)
                ],
                axis=1,
            )
            along_x = jnp.dot(plane_ref[...], window, preferred_element_type=f32)
            for b in range(2):
                for e in range(channels):
                    out_ref[o + i + b, e] = (
                        along_x[e * slab : (e + 1) * slab, b * cells : (b + 1) * cells]
                        + along_z[
                            (i + b) * slab : (i + b + 1) * slab, e * cells : (e + 1) * cells
                        ]
                    )
        return carry

    lax.fori_loop(0, orbs // CHUNK, chunk, 0)


def applied_body(
    piece,
    table_ref,
    kinetic_ref,
    potential_ref,
    adjoint_ref,
    out_ref,
    scratch,
):
    orbs, channels, slab, cells = kinetic_ref.shape
    channels -= 1
    rows = channels * slab
    pitch = scratch.shape[1] // orbs
    plane = lax.axis_index("comp") * slab + lax.broadcasted_iota(jnp.int32, (slab, cells), 0)
    fine = fine_cells(table_ref, slab, cells)
    potential = potential_ref[...]

    def chunk(k, carry):
        o = pl.multiple_of(k * CHUNK, CHUNK)
        weighted = (potential[None] * kinetic_ref[pl.ds(o, CHUNK), channels]).astype(bf16)
        back = jnp.dot(
            weighted.reshape(CHUNK * slab, cells), adjoint_ref[...], preferred_element_type=f32
        )
        for i in range(CHUNK):
            least, limit = region(table_ref, orbs, o + i)
            inside = (plane >= least) & (plane < limit)
            both = inside & fine
            for e in range(channels):
                keep = inside if e == 0 else both
                value = (
                    kinetic_ref[o + i, e]
                    + back[i * slab : (i + 1) * slab, e * cells : (e + 1) * cells]
                )
                spread(scratch, (o + i) * pitch + e * slab, jnp.where(keep, value, 0.0))
        return carry

    lax.fori_loop(0, orbs // CHUNK, chunk, 0)
    pack(scratch, out_ref, orbs, rows, piece)


def unpack(got_ref, rows_ref):
    sources = got_ref.shape[0]
    orbs = rows_ref.shape[0] // sources
    for i in range(sources):
        for g in range(rows_ref.shape[1] // LANES):
            rows_ref[pl.ds(i * orbs, orbs), pl.ds(g * LANES, LANES)] = got_ref[
                i, g * orbs : (g + 1) * orbs, :
            ]


def gram_halves(left_ref, right_ref, kept_ref, sent_ref):
    half = kept_ref.shape[0]
    mine = lax.axis_index("comp") % 2
    for place, ref in ((mine, kept_ref), (1 - mine, sent_ref)):
        row = pl.multiple_of(place * half, half)
        ref[...] = lax.dot_general(
            left_ref[pl.ds(row, half), :],
            right_ref[...],
            (((1,), (1,)), ((), ())),
            preferred_element_type=f32,
        ).astype(ref.dtype)


def self_gram_body(got_ref, rows_ref, kept_ref, sent_ref):
    unpack(got_ref, rows_ref)
    gram_halves(rows_ref, rows_ref, kept_ref, sent_ref)


def cross_gram_body(got_ref, other_ref, rows_ref, kept_ref, sent_ref):
    unpack(got_ref, rows_ref)
    gram_halves(rows_ref, other_ref, kept_ref, sent_ref)


def update_body(masked_ref, applied_ref, lagrange_ref, inter_ref, out_ref):
    masked = masked_ref[...]
    gradient = applied_ref[...].astype(f32) - jnp.dot(
        lagrange_ref[...], masked, preferred_element_type=f32
    )
    trial = (masked.astype(f32) - step_length * gradient).astype(bf16)
    following = 1.5 * trial.astype(f32) - 0.5 * jnp.dot(
        inter_ref[...], trial, preferred_element_type=f32
    )
    out_ref[...] = following.astype(bf16).T


def swap(value, axis, bit):
    count = lax.axis_size(axis)
    return lax.ppermute(value, axis, [(i, i ^ bit) for i in range(count)])


def bits_of(axis):
    bit, bits = 1, []
    while bit < lax.axis_size(axis):
        bits.append(bit)
        bit *= 2
    return bits


def stages():
    comp, orb = bits_of("comp"), bits_of("orb")
    groups = [[("comp", comp[0])]]
    for index, bit in enumerate(comp[1:]):
        groups.append([("comp", bit), ("orb", orb[index])])
    return groups, [("orb", bit) for bit in orb[len(comp) - 1 :]]


def place(group):
    return sum(((lax.axis_index(a) // b) % 2) << k for k, (a, b) in enumerate(group))


def pass_on(value, group, distance):
    flips = {}
    for k, (axis, bit) in enumerate(group):
        if distance >> k & 1:
            flips[axis] = flips.get(axis, 0) ^ bit
    axes = tuple(a for a in ("orb", "comp") if a in flips)
    if len(axes) == 1:
        return swap(value, axes[0], flips[axes[0]])
    sizes = [lax.axis_size(a) for a in axes]
    pairs = []
    for i in range(sizes[0]):
        for j in range(sizes[1]):
            to = (i ^ flips[axes[0]], j ^ flips[axes[1]])
            pairs.append((i * sizes[1] + j, to[0] * sizes[1] + to[1]))
    return lax.ppermute(value, axes, pairs)


def add_partner(kept, sent):
    return kept + pass_on(sent, stages()[0][0], 1).astype(f32)


def share_out(value):
    for group in stages()[0][1:]:
        members = 1 << len(group)
        size = value.shape[0] // members
        me = place(group)
        sent = value.astype(bf16)
        total = lax.dynamic_slice_in_dim(value, me * size, size, 0)
        for distance in range(1, members):
            share = lax.dynamic_slice_in_dim(sent, (me ^ distance) * size, size, 0)
            total = total + pass_on(share, group, distance).astype(f32)
        value = total
    return value


def exchange(value, step):
    axis, bit = step
    sent = value.astype(bf16)
    return sent.astype(f32) + swap(sent, axis, bit).astype(f32)


def give_everywhere(value):
    for group in reversed(stages()[0]):
        members = 1 << len(group)
        size = value.shape[0]
        me = place(group)
        got = [value] + [pass_on(value, group, d) for d in range(1, members)]
        whole = jnp.zeros((members * size,) + value.shape[1:], value.dtype)
        for distance, block in enumerate(got):
            whole = lax.dynamic_update_slice_in_dim(whole, block, (me ^ distance) * size, 0)
        value = whole
    return value


def local(psi, region_start, region_len, fine_mask, occupation, kinetic_taps, magic_taps, external):
    orbs, channels, slab, cells = psi.shape
    orb_count = lax.axis_size("orb")
    comp_count = lax.axis_size("comp")
    orbitals = orbs * orb_count
    piece = cells // orb_count
    coefs = channels * slab * piece
    groups = coefs // LANES
    grid_cells = slab * comp_count * cells
    first_cell = lax.axis_index("orb") * piece
    fine = jnp.pad(fine_mask.T, ((0, 0), (0, orbitals - slab)))
    rows = [region_start[None], region_len[None], occupation[None], fine]
    table = jnp.concatenate(rows, axis=0)

    scratch = pltpu.VMEM((cells // LANES, orbs * (channels * slab + PAD), LANES), f32)
    body_rows = orbs * coefs // LANES
    extra = slab * (cells // LANES)
    magic_forward = magic_matrix(magic_taps, cells)
    packed_shape = (orb_count, body_rows + 2 * extra, LANES)
    masked, packed = pl.pallas_call(
        functools.partial(mask_body, piece),
        out_shape=(
            jax.ShapeDtypeStruct(psi.shape, bf16),
            jax.ShapeDtypeStruct(packed_shape, bf16),
        ),
        in_specs=[SMEM, VMEM, VMEM],
        out_specs=(VMEM, ANY),
        scratch_shapes=[
            scratch,
            pltpu.VMEM(packed_shape, bf16),
            pltpu.SemaphoreType.DMA((groups + 1,)),
        ],
        compiler_params=params(),
        name="mask_values_pack",
        cost_estimate=SMALL,
    )(table, psi, magic_forward)

    ends = comp_count - 1
    before = lax.ppermute(masked, "comp", [(i, i + 1) for i in range(ends)])
    after = lax.ppermute(masked, "comp", [(i + 1, i) for i in range(ends)])
    masked_got = lax.all_to_all(packed, "orb", split_axis=0, concat_axis=0, tiled=True)
    parts = masked_got[:, body_rows:].reshape(orb_count * 2, cells // LANES, slab, LANES)
    total = jnp.sum(parts.astype(f32), axis=0).transpose(1, 0, 2).reshape(slab, cells)
    potential = external - xc_factor * jnp.cbrt(total)
    density = lax.dynamic_slice_in_dim(total, first_cell, piece, 1)

    kinetic = pl.pallas_call(
        kinetic_body,
        out_shape=jax.ShapeDtypeStruct((orbs, channels + 1, slab, cells), f32),
        in_specs=[VMEM] * 6,
        out_specs=VMEM,
        compiler_params=params(),
        name="kinetic",
        cost_estimate=SMALL,
    )(
        masked,
        before,
        after,
        depth_matrix(kinetic_taps, cells),
        plane_matrix(kinetic_taps, slab),
        magic_forward,
    )

    packed_applied = pl.pallas_call(
        functools.partial(applied_body, piece),
        out_shape=jax.ShapeDtypeStruct((orb_count, body_rows, LANES), bf16),
        in_specs=[SMEM] + [VMEM] * 3,
        out_specs=VMEM,
        scratch_shapes=[scratch],
        compiler_params=params(),
        name="applied_pack",
        cost_estimate=SMALL,
    )(
        table,
        kinetic,
        potential,
        adjoint_matrix(magic_taps, cells),
    )
    applied_got = lax.all_to_all(packed_applied, "orb", split_axis=0, concat_axis=0, tiled=True)

    row_shape = jax.ShapeDtypeStruct((orbitals, coefs), bf16)
    kept_shape = jax.ShapeDtypeStruct((orbitals // 2, orbitals), f32)
    sent_shape = jax.ShapeDtypeStruct((orbitals // 2, orbitals), bf16)
    masked_rows, *inter_part = pl.pallas_call(
        self_gram_body,
        out_shape=(row_shape, kept_shape, sent_shape),
        in_specs=[VMEM],
        out_specs=(VMEM, VMEM, VMEM),
        compiler_params=params(),
        name="intersection",
        cost_estimate=SMALL,
    )(masked_got)
    inter = share_out(add_partner(*inter_part))
    for step in stages()[1][:-1]:
        inter = exchange(inter, step)

    applied_got, inter = lax.optimization_barrier((applied_got, inter))
    applied_rows, *lagrange_part = pl.pallas_call(
        cross_gram_body,
        out_shape=(row_shape, kept_shape, sent_shape),
        in_specs=[VMEM, VMEM],
        out_specs=(VMEM, VMEM, VMEM),
        compiler_params=params(),
        name="lagrange",
        cost_estimate=SMALL,
    )(applied_got, masked_rows)
    lagrange = share_out(add_partner(*lagrange_part))
    for step in stages()[1][:-1]:
        lagrange = exchange(lagrange, step)
    both = exchange(jnp.concatenate([lagrange, inter], axis=1), stages()[1][-1])
    both = give_everywhere((both / grid_cells).astype(bf16))

    width = 512
    following = pl.pallas_call(
        update_body,
        grid=(coefs // width,),
        out_shape=jax.ShapeDtypeStruct((coefs, orbitals), bf16),
        in_specs=[
            pl.BlockSpec((orbitals, width), lambda k: (0, k)),
            pl.BlockSpec((orbitals, width), lambda k: (0, k)),
            pl.BlockSpec((orbitals, orbitals), lambda k: (0, 0)),
            pl.BlockSpec((orbitals, orbitals), lambda k: (0, 1)),
        ],
        out_specs=pl.BlockSpec((width, orbitals), lambda k: (k, 0)),
        compiler_params=params(),
        name="update",
        cost_estimate=SMALL,
    )(masked_rows, applied_rows, both, both)
    psi_next = following.reshape(channels, slab, piece, orbitals).transpose(3, 0, 1, 2)
    return (density, psi_next)


def solution(mesh):
    return jax.shard_map(
        local,
        mesh=mesh,
        in_specs=(
            P("orb", None, "comp", None),
            P(),
            P(),
            P("comp", None),
            P(),
            P(),
            P(),
            P("comp", None),
        ),
        out_specs=(P("comp", "orb"), P(None, None, "comp", "orb")),
        check_vma=False,
    )
```

```python
import functools

import jax
import jax.numpy as jnp
from jax import lax
from jax.experimental import pallas as pl
from jax.experimental.pallas import tpu as pltpu
from jax.sharding import PartitionSpec as P

ZB = 16
LANES = 128
CHUNK = 16
PAD = 8

xc_factor = 0.98474502
step_length = 0.1
f32 = jnp.float32
bf16 = jnp.bfloat16
VMEM = pl.BlockSpec(memory_space=pltpu.VMEM)
ANY = pl.BlockSpec(memory_space=pl.ANY)
SMEM = pl.BlockSpec(memory_space=pltpu.SMEM)


SMALL = pl.CostEstimate(flops=1024, bytes_accessed=1024, transcendentals=0)


def params(mib=20):
    return pltpu.CompilerParams(vmem_limit_bytes=mib * 2**20)


def band(window, length, shift, sign, taps):
    count = taps.shape[0]
    offset = sign * (jnp.arange(window)[:, None] - jnp.arange(length)[None, :]) + shift
    onehot = (offset[:, :, None] == jnp.arange(count)[None, None, :]).astype(bf16)
    return onehot


def depth_matrix(taps, cells):
    onehot = band(cells, cells, 14, 1, taps)
    kernel = jnp.einsum("jit,ted->djei", onehot, taps, preferred_element_type=f32).astype(bf16)
    ch = taps.shape[1]
    return kernel.reshape(ch * cells, ch * cells)


def plane_matrix(taps, slab):
    ch = taps.shape[1]
    parts = []
    for block in (-1, 0, 1):
        onehot = band(slab, slab, 14 + block * slab, 1, taps)
        part = jnp.einsum("jit,ted->eidj", onehot, taps, preferred_element_type=f32).astype(bf16)
        parts.append(part.reshape(ch * slab, ch * slab))
    return jnp.concatenate(parts, axis=1)


def magic_matrix(magic, cells):
    onehot = band(cells, cells, 7, 1, magic)
    kernel = jnp.einsum("jit,td->dji", onehot, magic, preferred_element_type=f32).astype(bf16)
    return kernel.reshape(magic.shape[1] * cells, cells)


def adjoint_matrix(magic, cells):
    onehot = band(cells, cells, 7, -1, magic)
    kernel = jnp.einsum("jit,te->jei", onehot, magic, preferred_element_type=f32).astype(bf16)
    return kernel.reshape(cells, magic.shape[1] * cells)


def spread(scratch, row, value):
    slab = value.shape[0]
    for tile in range(value.shape[1] // LANES):
        scratch[tile, pl.ds(pl.multiple_of(row, 8), slab), :] = value[
            :, tile * LANES : (tile + 1) * LANES
        ]


def pack(scratch, staged, orbs, rows, piece, copies=None):
    pieces = staged.shape[0]
    blocks = LANES // piece
    pitch = scratch.shape[1] // orbs
    lane = lax.broadcasted_iota(jnp.int32, (CHUNK, LANES), 1) // piece

    def group(g, carry):
        for tile in range(pieces // blocks):
            for start in range(0, orbs, CHUNK):
                held = [
                    scratch[
                        tile, pl.ds(start * pitch + g * blocks + c, CHUNK, stride=pitch), :
                    ].astype(bf16)
                    for c in range(blocks)
                ]
                bit = 1
                while bit < blocks:
                    low_lane = (lane & bit) == 0
                    for c in range(blocks):
                        if c & bit:
                            continue
                        low, high = held[c], held[c | bit]
                        held[c] = jnp.where(low_lane, low, pltpu.roll(high, bit * piece, 1))
                        held[c | bit] = jnp.where(
                            low_lane, pltpu.roll(low, LANES - bit * piece, 1), high
                        )
                    bit *= 2
                for c in range(blocks):
                    row = pl.multiple_of(g * orbs + start, CHUNK)
                    staged[tile * blocks + c, pl.ds(row, CHUNK), :] = held[c]
        if copies:
            leave(g).start()
        return carry

    def leave(g):
        out_ref, sems = copies
        share = pl.ds(pl.multiple_of(g * orbs, CHUNK), orbs)
        return pltpu.make_async_copy(
            staged.at[:, share, :], out_ref.at[:, share, :], sems.at[g]
        )

    def finish(g, carry):
        leave(g).wait()
        return carry

    lax.fori_loop(0, rows // blocks, group, 0)
    if copies:
        lax.fori_loop(0, rows // blocks, finish, 0)


def fine_cells(table_ref, slab, cells):
    x = lax.broadcasted_iota(jnp.int32, (slab, LANES), 0)
    block = lax.broadcasted_iota(jnp.int32, (slab, LANES), 1) // ZB
    tiles = []
    for tile in range(cells // LANES):
        held = jnp.zeros((slab, LANES), jnp.int32)
        for b in range(LANES // ZB):
            for p in range(slab):
                bit = table_ref[3 + tile * (LANES // ZB) + b, p]
                held = jnp.where((x == p) & (block == b), bit, held)
        tiles.append(held)
    return jnp.concatenate(tiles, axis=1) > 0


def region(table_ref, orbs, o):
    spot = lax.axis_index("orb") * orbs + o
    return table_ref[0, spot], table_ref[0, spot] + table_ref[1, spot]


def mask_body(
    piece,
    table_ref,
    psi_ref,
    magic_ref,
    masked_ref,
    out_ref,
    scratch,
    staged,
    sems,
):
    orbs, channels, slab, cells = psi_ref.shape
    rows = channels * slab
    pitch = scratch.shape[1] // orbs

    first_orbital = lax.axis_index("orb") * orbs
    plane = lax.axis_index("comp") * slab + lax.broadcasted_iota(jnp.int32, (slab, cells), 0)
    fine = fine_cells(table_ref, slab, cells)

    def chunk(k, total):
        o = pl.multiple_of(k * CHUNK, CHUNK)
        for i in range(CHUNK):
            least, limit = region(table_ref, orbs, o + i)
            inside = (plane >= least) & (plane < limit)
            both = inside & fine
            for e in range(channels):
                keep = inside if e == 0 else both
                value = jnp.where(keep, psi_ref[o + i, e].astype(f32), 0.0)
                masked_ref[o + i, e] = value.astype(bf16)
                spread(scratch, (o + i) * pitch + e * slab, value)
        lhs = jnp.concatenate(
            [
                masked_ref[pl.ds(o, CHUNK), d].reshape(CHUNK * slab, cells)
                for d in range(channels)
            ],
            axis=1,
        )
        result = jnp.dot(lhs, magic_ref[...], preferred_element_type=f32)
        for i in range(CHUNK):
            part = result[i * slab : (i + 1) * slab]
            total = total + table_ref[2, first_orbital + o + i].astype(f32) * part * part
        return total

    density = lax.fori_loop(0, orbs // CHUNK, chunk, jnp.zeros((slab, cells), f32))
    coarse = density.astype(bf16)
    rest = (density - coarse.astype(f32)).astype(bf16)
    body = orbs * rows * piece // LANES
    for j in range(staged.shape[0]):
        row = body
        for part in (coarse, rest):
            for tile in range(cells // LANES):
                staged[j, row : row + slab, :] = part[:, tile * LANES : (tile + 1) * LANES]
                row += slab
    extra = pltpu.make_async_copy(
        staged.at[:, body:, :], out_ref.at[:, body:, :], sems.at[rows * piece // LANES]
    )
    extra.start()
    pack(scratch, staged, orbs, rows, piece, (out_ref, sems))
    extra.wait()


def kinetic_body(
    masked_ref, before_ref, after_ref, depth_ref, plane_ref, magic_ref, out_ref
):
    orbs, channels, slab, cells = masked_ref.shape
    rows = channels * slab

    def chunk(k, carry):
        o = pl.multiple_of(k * CHUNK, CHUNK)
        lhs = jnp.concatenate(
            [
                masked_ref[pl.ds(o, CHUNK), d].reshape(CHUNK * slab, cells)
                for d in range(channels)
            ],
            axis=1,
        )
        along_z = jnp.dot(lhs, depth_ref[...], preferred_element_type=f32)
        out_ref[pl.ds(o, CHUNK), channels] = jnp.dot(
            lhs, magic_ref[...], preferred_element_type=f32
        ).reshape(CHUNK, slab, cells)
        for i in range(0, CHUNK, 2):
            window = jnp.concatenate(
                [
                    jnp.concatenate(
                        [
                            ref[o + i + b].reshape(rows, cells)
                            for ref in (before_ref, masked_ref, after_ref)
                        ],
                        axis=0,
                    )
                    for b in range(2)
                ],
                axis=1,
            )
            along_x = jnp.dot(plane_ref[...], window, preferred_element_type=f32)
            for b in range(2):
                for e in range(channels):
                    out_ref[o + i + b, e] = (
                        along_x[e * slab : (e + 1) * slab, b * cells : (b + 1) * cells]
                        + along_z[
                            (i + b) * slab : (i + b + 1) * slab, e * cells : (e + 1) * cells
                        ]
                    )
        return carry

    lax.fori_loop(0, orbs // CHUNK, chunk, 0)


def applied_body(
    piece,
    table_ref,
    kinetic_ref,
    potential_ref,
    adjoint_ref,
    out_ref,
    scratch,
):
    orbs, channels, slab, cells = kinetic_ref.shape
    channels -= 1
    rows = channels * slab
    pitch = scratch.shape[1] // orbs
    plane = lax.axis_index("comp") * slab + lax.broadcasted_iota(jnp.int32, (slab, cells), 0)
    fine = fine_cells(table_ref, slab, cells)
    potential = potential_ref[...]

    def chunk(k, carry):
        o = pl.multiple_of(k * CHUNK, CHUNK)
        weighted = (potential[None] * kinetic_ref[pl.ds(o, CHUNK), channels]).astype(bf16)
        back = jnp.dot(
            weighted.reshape(CHUNK * slab, cells), adjoint_ref[...], preferred_element_type=f32
        )
        for i in range(CHUNK):
            least, limit = region(table_ref, orbs, o + i)
            inside = (plane >= least) & (plane < limit)
            both = inside & fine
            for e in range(channels):
                keep = inside if e == 0 else both
                value = (
                    kinetic_ref[o + i, e]
                    + back[i * slab : (i + 1) * slab, e * cells : (e + 1) * cells]
                )
                spread(scratch, (o + i) * pitch + e * slab, jnp.where(keep, value, 0.0))
        return carry

    lax.fori_loop(0, orbs // CHUNK, chunk, 0)
    pack(scratch, out_ref, orbs, rows, piece)


def unpack(got_ref, rows_ref):
    sources = got_ref.shape[0]
    orbs = rows_ref.shape[0] // sources
    for i in range(sources):
        for g in range(rows_ref.shape[1] // LANES):
            rows_ref[pl.ds(i * orbs, orbs), pl.ds(g * LANES, LANES)] = got_ref[
                i, g * orbs : (g + 1) * orbs, :
            ]


def gram_halves(left_ref, right_ref, kept_ref, sent_ref):
    half = kept_ref.shape[0]
    mine = lax.axis_index("comp") % 2
    for place, ref in ((mine, kept_ref), (1 - mine, sent_ref)):
        row = pl.multiple_of(place * half, half)
        ref[...] = lax.dot_general(
            left_ref[pl.ds(row, half), :],
            right_ref[...],
            (((1,), (1,)), ((), ())),
            preferred_element_type=f32,
        ).astype(ref.dtype)


def self_gram_body(got_ref, rows_ref, kept_ref, sent_ref):
    unpack(got_ref, rows_ref)
    gram_halves(rows_ref, rows_ref, kept_ref, sent_ref)


def cross_gram_body(got_ref, other_ref, rows_ref, kept_ref, sent_ref):
    unpack(got_ref, rows_ref)
    gram_halves(rows_ref, other_ref, kept_ref, sent_ref)


def update_body(masked_ref, applied_ref, lagrange_ref, inter_ref, out_ref):
    masked = masked_ref[...]
    gradient = applied_ref[...].astype(f32) - jnp.dot(
        lagrange_ref[...], masked, preferred_element_type=f32
    )
    trial = (masked.astype(f32) - step_length * gradient).astype(bf16)
    following = 1.5 * trial.astype(f32) - 0.5 * jnp.dot(
        inter_ref[...], trial, preferred_element_type=f32
    )
    out_ref[...] = following.astype(bf16).T


def swap(value, axis, bit):
    count = lax.axis_size(axis)
    return lax.ppermute(value, axis, [(i, i ^ bit) for i in range(count)])


def bits_of(axis):
    bit, bits = 1, []
    while bit < lax.axis_size(axis):
        bits.append(bit)
        bit *= 2
    return bits


def stages():
    comp, orb = bits_of("comp"), bits_of("orb")
    groups = [[("comp", comp[0])]]
    for index, bit in enumerate(comp[1:]):
        groups.append([("comp", bit), ("orb", orb[index])])
    return groups, [("orb", bit) for bit in orb[len(comp) - 1 :]]


def place(group):
    return sum(((lax.axis_index(a) // b) % 2) << k for k, (a, b) in enumerate(group))


def pass_on(value, group, distance):
    flips = {}
    for k, (axis, bit) in enumerate(group):
        if distance >> k & 1:
            flips[axis] = flips.get(axis, 0) ^ bit
    axes = tuple(a for a in ("orb", "comp") if a in flips)
    if len(axes) == 1:
        return swap(value, axes[0], flips[axes[0]])
    sizes = [lax.axis_size(a) for a in axes]
    pairs = []
    for i in range(sizes[0]):
        for j in range(sizes[1]):
            to = (i ^ flips[axes[0]], j ^ flips[axes[1]])
            pairs.append((i * sizes[1] + j, to[0] * sizes[1] + to[1]))
    return lax.ppermute(value, axes, pairs)


def add_partner(kept, sent):
    return kept + pass_on(sent, stages()[0][0], 1).astype(f32)


def share_out(value):
    for group in stages()[0][1:]:
        members = 1 << len(group)
        size = value.shape[0] // members
        me = place(group)
        sent = value.astype(bf16)
        total = lax.dynamic_slice_in_dim(value, me * size, size, 0)
        for distance in range(1, members):
            share = lax.dynamic_slice_in_dim(sent, (me ^ distance) * size, size, 0)
            total = total + pass_on(share, group, distance).astype(f32)
        value = total
    return value


def exchange(value, step):
    axis, bit = step
    sent = value.astype(bf16)
    return sent.astype(f32) + swap(sent, axis, bit).astype(f32)


def give_everywhere(value):
    for group in reversed(stages()[0]):
        members = 1 << len(group)
        size = value.shape[0]
        me = place(group)
        got = [value] + [pass_on(value, group, d) for d in range(1, members)]
        whole = jnp.zeros((members * size,) + value.shape[1:], value.dtype)
        for distance, block in enumerate(got):
            whole = lax.dynamic_update_slice_in_dim(whole, block, (me ^ distance) * size, 0)
        value = whole
    return value


def local(psi, region_start, region_len, fine_mask, occupation, kinetic_taps, magic_taps, external):
    orbs, channels, slab, cells = psi.shape
    orb_count = lax.axis_size("orb")
    comp_count = lax.axis_size("comp")
    orbitals = orbs * orb_count
    piece = cells // orb_count
    coefs = channels * slab * piece
    groups = coefs // LANES
    grid_cells = slab * comp_count * cells
    first_cell = lax.axis_index("orb") * piece
    fine = jnp.pad(fine_mask.T, ((0, 0), (0, orbitals - slab)))
    rows = [region_start[None], region_len[None], occupation[None], fine]
    table = jnp.concatenate(rows, axis=0)

    scratch = pltpu.VMEM((cells // LANES, orbs * (channels * slab + PAD), LANES), f32)
    body_rows = orbs * coefs // LANES
    extra = slab * (cells // LANES)
    magic_forward = magic_matrix(magic_taps, cells)
    packed_shape = (orb_count, body_rows + 2 * extra, LANES)
    masked, packed = pl.pallas_call(
        functools.partial(mask_body, piece),
        out_shape=(
            jax.ShapeDtypeStruct(psi.shape, bf16),
            jax.ShapeDtypeStruct(packed_shape, bf16),
        ),
        in_specs=[SMEM, VMEM, VMEM],
        out_specs=(VMEM, ANY),
        scratch_shapes=[
            scratch,
            pltpu.VMEM(packed_shape, bf16),
            pltpu.SemaphoreType.DMA((groups + 1,)),
        ],
        compiler_params=params(),
        name="mask_values_pack",
        cost_estimate=SMALL,
    )(table, psi, magic_forward)

    ends = comp_count - 1
    before = lax.ppermute(masked, "comp", [(i, i + 1) for i in range(ends)])
    after = lax.ppermute(masked, "comp", [(i + 1, i) for i in range(ends)])
    masked_got = lax.all_to_all(packed, "orb", split_axis=0, concat_axis=0, tiled=True)
    parts = masked_got[:, body_rows:].reshape(orb_count * 2, cells // LANES, slab, LANES)
    total = jnp.sum(parts.astype(f32), axis=0).transpose(1, 0, 2).reshape(slab, cells)
    potential = external - xc_factor * jnp.cbrt(total)
    density = lax.dynamic_slice_in_dim(total, first_cell, piece, 1)

    kinetic = pl.pallas_call(
        kinetic_body,
        out_shape=jax.ShapeDtypeStruct((orbs, channels + 1, slab, cells), f32),
        in_specs=[VMEM] * 6,
        out_specs=VMEM,
        compiler_params=params(),
        name="kinetic",
        cost_estimate=SMALL,
    )(
        masked,
        before,
        after,
        depth_matrix(kinetic_taps, cells),
        plane_matrix(kinetic_taps, slab),
        magic_forward,
    )

    packed_applied = pl.pallas_call(
        functools.partial(applied_body, piece),
        out_shape=jax.ShapeDtypeStruct((orb_count, body_rows, LANES), bf16),
        in_specs=[SMEM] + [VMEM] * 3,
        out_specs=VMEM,
        scratch_shapes=[scratch],
        compiler_params=params(),
        name="applied_pack",
        cost_estimate=SMALL,
    )(
        table,
        kinetic,
        potential,
        adjoint_matrix(magic_taps, cells),
    )
    applied_got = lax.all_to_all(packed_applied, "orb", split_axis=0, concat_axis=0, tiled=True)

    row_shape = jax.ShapeDtypeStruct((orbitals, coefs), bf16)
    kept_shape = jax.ShapeDtypeStruct((orbitals // 2, orbitals), f32)
    sent_shape = jax.ShapeDtypeStruct((orbitals // 2, orbitals), bf16)
    masked_rows, *inter_part = pl.pallas_call(
        self_gram_body,
        out_shape=(row_shape, kept_shape, sent_shape),
        in_specs=[VMEM],
        out_specs=(VMEM, VMEM, VMEM),
        compiler_params=params(),
        name="intersection",
        cost_estimate=SMALL,
    )(masked_got)
    inter = share_out(add_partner(*inter_part))
    for step in stages()[1][:-1]:
        inter = exchange(inter, step)

    applied_got, inter = lax.optimization_barrier((applied_got, inter))
    applied_rows, *lagrange_part = pl.pallas_call(
        cross_gram_body,
        out_shape=(row_shape, kept_shape, sent_shape),
        in_specs=[VMEM, VMEM],
        out_specs=(VMEM, VMEM, VMEM),
        compiler_params=params(),
        name="lagrange",
        cost_estimate=SMALL,
    )(applied_got, masked_rows)
    lagrange = add_partner(*lagrange_part)
    inter = exchange(lax.optimization_barrier((inter, lagrange))[0], stages()[1][-1])
    lagrange = share_out(lagrange)
    for step in stages()[1]:
        lagrange = exchange(lagrange, step)
    both = jnp.concatenate([lagrange, inter], axis=1)
    both = give_everywhere((both / grid_cells).astype(bf16))

    width = coefs
    following = pl.pallas_call(
        update_body,
        grid=(coefs // width,),
        out_shape=jax.ShapeDtypeStruct((coefs, orbitals), bf16),
        in_specs=[
            pl.BlockSpec((orbitals, width), lambda k: (0, k)),
            pl.BlockSpec((orbitals, width), lambda k: (0, k)),
            pl.BlockSpec((orbitals, orbitals), lambda k: (0, 0)),
            pl.BlockSpec((orbitals, orbitals), lambda k: (0, 1)),
        ],
        out_specs=pl.BlockSpec((width, orbitals), lambda k: (k, 0)),
        compiler_params=params(),
        name="update",
        cost_estimate=SMALL,
    )(masked_rows, applied_rows, both, both)
    psi_next = following.reshape(channels, slab, piece, orbitals).transpose(3, 0, 1, 2)
    return (density, psi_next)


def solution(mesh):
    return jax.shard_map(
        local,
        mesh=mesh,
        in_specs=(
            P("orb", None, "comp", None),
            P(),
            P(),
            P("comp", None),
            P(),
            P(),
            P(),
            P("comp", None),
        ),
        out_specs=(P("comp", "orb"), P(None, None, "comp", "orb")),
        check_vma=False,
    )
```
